512 devices in a mesh: ctxlo: 16 (over x_hi, z), ctxhi: 32 (over y, x_lo, core).
Axes of the slice: x: 4 (x_hi: 2, x_lo: 2; x = x_hi * 2 + x_lo), y: 8, z: 8, core: 2. Of those that a mesh axis runs over, the one named last changes fastest.
Arguments:
- query_matrix: float32 [131072, 1536], P(('ctxhi', 'ctxlo')), may hold values from -6 to 6
- key_matrix: float32 [131072, 256], P(('ctxhi', 'ctxlo')), may hold values from -6 to 6
- value_matrix: float32 [131072, 256], P(('ctxhi', 'ctxlo')), may hold values from -24 to 24
- block_lists: int32 [1024, 15], P(('ctxhi', 'ctxlo')), may hold values from -1 to 1023, as said below
Outputs:
- attended: float32 [131072, 1536], P(('ctxhi', 'ctxlo'))
The draws below stay inside these ranges and needn't reach their ends.
Inputs may be any that keep to these rules, and one draw needn't show every extreme that they name: `block_lists`: row q holds distinct key blocks, each one of q, q - 1, q - 2, q - 3 and q - 2**j for j >= 2, never below 0, always including q itself, in any order; the other slots hold -1.
All inputs are finite; a program needn't handle non-finite values.
Results may differ from the reference program's by a relative error of at most 0.0003.
Values sent between devices are 32-bit elements; how exact they have to be, the bound alone decides.
A program may use at most 64 MiB of HBM per device.

```python
import jax
import jax.numpy as jnp
from jax import lax

QUERY_HEADS = 12
KEY_VALUE_HEADS = 2
HEAD_FEATURES = 128
BLOCK_TOKENS = 128
LIST_SLOTS = 15
SEQUENCE_TOKENS = 131072
SEQUENCE_BLOCKS = 1024


def draw_key_matrix(key, part):
    return jnp.clip(jax.random.normal(jax.random.fold_in(key, 21), (SEQUENCE_TOKENS, KEY_VALUE_HEADS * HEAD_FEATURES), jnp.float32), -6.0, 6.0)


def draw_query_matrix(key, part):
    return jnp.clip(1.5 * jax.random.normal(jax.random.fold_in(key, 31), (SEQUENCE_TOKENS, QUERY_HEADS * HEAD_FEATURES), jnp.float32), -6.0, 6.0)


def draw_block_lists(key, part):
    slot_index = jnp.arange(LIST_SLOTS, dtype=jnp.int32)[None, :]
    query_block_index = jnp.arange(SEQUENCE_BLOCKS, dtype=jnp.int32)[:, None]
    distance = jnp.where(slot_index < 4, slot_index, jnp.left_shift(jnp.int32(1), jnp.maximum(slot_index - 2, 0)))
    target = query_block_index - distance
    kept_slots = (jax.random.randint(jax.random.fold_in(key, 41), (SEQUENCE_BLOCKS, LIST_SLOTS), 0, 4) < 3) | (slot_index == 0)
    entries = jnp.where(kept_slots & (target >= 0), target, -1)
    order_key = jax.random.randint(jax.random.fold_in(key, 42), (SEQUENCE_BLOCKS, LIST_SLOTS), 0, 1 << 20) * LIST_SLOTS + slot_index
    shuffle = jnp.argsort(order_key, axis=1)
    return jnp.take_along_axis(entries, shuffle, axis=1).astype(jnp.int32)


def block_levels(rng, shape, cuts, low, high):
    gain, own = 1.0, jax.random.fold_in(rng, 6)
    for position, parts in cuts:
        draws = jnp.exp(jax.random.uniform(jax.random.fold_in(own, position), (parts,), jnp.float32, low / len(cuts), high / len(cuts)))
        gain = gain * jnp.repeat(draws, shape[position] // parts).reshape([-1 if axis == position else 1 for axis in range(len(shape))])
    return gain


def normal_values(rng, dims, deviation, bound, split=(), kind=jnp.bfloat16):
    values = deviation * jax.random.normal(rng, dims, jnp.float32)
    if split:
        values = values * block_levels(rng, dims, split, -0.22, 0.18)
    return jnp.clip(values, -bound, bound).astype(kind)


def setup_inputs(seed: int = 0) -> dict:
    seeds = jax.random.split(jax.random.key(seed), 5)
    query_matrix = draw_query_matrix(jax.random.fold_in(seeds[4], 71), 0)
    key_matrix = draw_key_matrix(jax.random.fold_in(seeds[4], 71), 0)
    value_matrix = normal_values(seeds[2], (SEQUENCE_TOKENS, KEY_VALUE_HEADS * HEAD_FEATURES), 4.0, 24.0, ((0, 512),), jnp.float32)
    block_lists = draw_block_lists(jax.random.fold_in(seeds[4], 71), 0)
    return {"query_matrix": query_matrix, "key_matrix": key_matrix, "value_matrix": value_matrix, "block_lists": block_lists}


def reference(query_matrix, key_matrix, value_matrix, block_lists):
    group_width = QUERY_HEADS // KEY_VALUE_HEADS
    score_scale = HEAD_FEATURES ** -0.5
    key_block_tiles = key_matrix.reshape(SEQUENCE_BLOCKS, BLOCK_TOKENS, KEY_VALUE_HEADS, HEAD_FEATURES)
    value_block_tiles = value_matrix.reshape(SEQUENCE_BLOCKS, BLOCK_TOKENS, KEY_VALUE_HEADS, HEAD_FEATURES)
    within = jnp.arange(BLOCK_TOKENS, dtype=jnp.int32)

    def one_block(query_block_index):
        query_portion = lax.dynamic_slice_in_dim(query_matrix, query_block_index * BLOCK_TOKENS, BLOCK_TOKENS, 0).reshape(BLOCK_TOKENS, KEY_VALUE_HEADS, group_width, HEAD_FEATURES)
        listed = block_lists[query_block_index]
        clamped_blocks = jnp.maximum(listed, 0).astype(jnp.int32)
        key_portion = key_block_tiles[clamped_blocks].reshape(LIST_SLOTS * BLOCK_TOKENS, KEY_VALUE_HEADS, HEAD_FEATURES)
        value_portion = value_block_tiles[clamped_blocks].reshape(LIST_SLOTS * BLOCK_TOKENS, KEY_VALUE_HEADS, HEAD_FEATURES)
        key_pos = (clamped_blocks[:, None] * BLOCK_TOKENS + within[None, :]).reshape(LIST_SLOTS * BLOCK_TOKENS)
        valid_keys = jnp.repeat(listed >= 0, BLOCK_TOKENS)
        query_pos = query_block_index * BLOCK_TOKENS + within
        allowed = valid_keys[None, :] & (key_pos[None, :] <= query_pos[:, None])
        scores = jnp.einsum("rhgd,khd->hgrk", query_portion, key_portion, precision=lax.Precision.HIGHEST) * score_scale
        scores = jnp.where(allowed[None, None], scores, -jnp.inf)
        row_max = jnp.max(scores, axis=3, keepdims=True)
        weights = jnp.exp(scores - row_max)
        denominator = jnp.sum(weights, axis=3)
        weighted = jnp.einsum("hgrk,khd->rhgd", weights, value_portion, precision=lax.Precision.HIGHEST)
        return (weighted / jnp.transpose(denominator, (2, 0, 1))[..., None]).reshape(BLOCK_TOKENS, QUERY_HEADS * HEAD_FEATURES)

    result = lax.map(one_block, jnp.arange(SEQUENCE_BLOCKS, dtype=jnp.int32))
    return result.reshape(SEQUENCE_BLOCKS * BLOCK_TOKENS, QUERY_HEADS * HEAD_FEATURES)
```

```python
import jax
import jax.numpy as jnp
from jax import lax
from jax.experimental import pallas as pl
from jax.experimental.pallas import tpu as pltpu
from jax.sharding import PartitionSpec as P

HEADS, GROUPS, FEATURES, BLOCK = 12, 2, 128, 128
PER_GROUP = HEADS // GROUPS
SLOTS = 15
ROWS, COLS = 256, 512
OFFSETS = (1, 2, 4, 8, 16, 32, 64, 128, 256)
OWN = 0
SLOT = {o: i + 1 for i, o in enumerate(OFFSETS)}
RELAY_Z, RELAY_Y = 10, 11
BUFFERS = 12
RULES = ("1", "2", "2b", "4", "4f", "4a", "8", "16", "32", "64", "128", "256", "256a")
CHUNKS = 8
CHUNK = ROWS // CHUNKS
STAGES = (("64", 0), ("8", 0), ("1", 1), ("y", 3), ("128", 2), ("2", 3), ("z", 5))
NEG = -1e30
MESH = pl.DeviceIdType.MESH

STEPS = (
    (((0, 0), (8, 0)), ((1, 0), (1, 1)), ((16, 0), (32, 0)), ((64, 0), (128, 0)), ((2, 0), (2, 1)), ((4, 0), (256, 0))),
    (((0, 0), (0, 1)), ((1, 0), (1, 1)), ((8, 1), (16, 1)), ((32, 1), (64, 1)), ((2, 1), (128, 1)), ((4, 1), (256, 1))),
)


def pick(index, values):
    out = jnp.int32(values[0])
    for i, v in enumerate(values[1:], 1):
        if v != values[i - 1]:
            out = jnp.where(index >= i, jnp.int32(v), out)
    return out


def split(a):
    hi = a.astype(jnp.bfloat16)
    return hi, (a - hi.astype(jnp.float32)).astype(jnp.bfloat16)


def kernel(q_ref, k_ref, v_ref, lists_ref, out_ref, buf, q_vmem, q_cat, acc, top, total, ssem, rsem, lsem):
    lo, hi = lax.axis_index("ctxlo"), lax.axis_index("ctxhi")
    h, z = lo // 8, lo % 8
    y, g, c = hi // 4, (hi // 2) % 2, hi % 2
    x = h * 2 + g
    shard = hi * 16 + lo

    def dev(dy, dx, dz, core):
        xx = (x + dx + 4) % 4
        return {"ctxlo": (xx // 2) * 8 + (z + dz + 8) % 8, "ctxhi": ((y + dy + 8) % 8) * 4 + (xx % 2) * 2 + core}

    k_copy = pltpu.make_async_copy(k_ref, buf.at[OWN, :, pl.ds(0, 256)], lsem.at[0])
    v_copy = pltpu.make_async_copy(v_ref, buf.at[OWN, :, pl.ds(256, 256)], lsem.at[1])
    q_copy = pltpu.make_async_copy(q_ref, q_vmem, lsem.at[2])
    k_copy.start()
    v_copy.start()
    q_copy.start()
    barrier = pltpu.get_barrier_semaphore()
    f = 1 - c
    peers = [dev(0, 0, 1, c), dev(0, 0, -1, c), dev(0, 0, 2, c), dev(0, 0, -2, c), dev(1, 0, 0, c), dev(-1, 0, 0, c),
             dev(2, 0, 0, c), dev(-2, 0, 0, c), dev(0, 1, 0, c), dev(0, -1, 0, c), dev(0, 1, 0, f), dev(0, -1, 0, f),
             dev(0, 2, 0, c), dev(0, 2, 0, f), dev(0, 0, 0, f)]
    for peer in peers:
        pl.semaphore_signal(barrier, 1, device_id=peer, device_id_type=MESH)
    k_copy.wait()
    v_copy.wait()
    pl.semaphore_wait(barrier, len(peers))

    def rows(k):
        return pl.ds(pl.multiple_of(k * CHUNK, CHUNK), CHUNK)

    def send(rule, src, dst, k, target):
        return pltpu.make_async_remote_copy(
            src_ref=buf.at[src, rows(k)], dst_ref=buf.at[dst, rows(k)],
            send_sem=ssem.at[RULES.index(rule), k], recv_sem=rsem.at[dst, k],
            device_id=target, device_id_type=MESH)

    def arrive(dst, k):
        send("1", dst, dst, k, peers[0]).wait_recv()

    t1, tz2, tzm2 = peers[0], peers[2], peers[3]
    y1, y2, ym2 = peers[4], peers[6], peers[7]
    side = jnp.where(g == 0, 1, -1)
    t32 = dev(0, side, 0, c)
    t16 = dev(0, jnp.where(c == 0, 0, side), 0, f)
    top_x = h == 1
    carry = top_x & (c == 1)
    t8 = dev(0, jnp.where(carry, -side, 2), 0, jnp.where(top_x, f, c))
    g1 = g == 1
    y16 = g1 & (c == 1)
    y8 = g1 & carry
    z_minus = (z == 1) | (z == 3) | (z == 4) | (z == 5) | (z == 7)
    z_forward = (z == 7) | (z == 1) | (z == 2) | (z == 3) | (z == 5)
    z_plus = (z == 0) | (z == 2) | (z == 4)
    z_high = z >= 4
    y_odd = y % 2 == 1
    no = jnp.logical_not

    def when(condition, action):
        pl.when(condition)(action)

    def first(k, _):
        send("64", OWN, SLOT[64], k, y1).start()
        when(no(y8), lambda: send("8", OWN, SLOT[8], k, t8).start())
        when(z < 7, lambda: send("1", OWN, SLOT[1], k, t1).start())
        when(no(g1), lambda: send("32", OWN, SLOT[32], k, t32).start())
        when(no(y16), lambda: send("16", OWN, SLOT[16], k, t16).start())
        when(z_minus & no(z_high), lambda: send("4a", OWN, RELAY_Z, k, tzm2).start())
        when(y_odd, lambda: send("256a", OWN, RELAY_Y, k, ym2).start())
        return 0

    lax.fori_loop(0, CHUNKS, first, 0)

    def s64(k):
        arrive(SLOT[64], k)
        send("128", SLOT[64], SLOT[128], k, y1).start()
        when(y8, lambda: send("8", SLOT[64], SLOT[8], k, t8).start())
        when(g1, lambda: send("32", SLOT[64], SLOT[32], k, t32).start())
        when(y16, lambda: send("16", SLOT[64], SLOT[16], k, t16).start())

    def s8(k):
        arrive(SLOT[8], k)
        when(z == 7, lambda: send("1", SLOT[8], SLOT[1], k, t1).start())
        when(z == 6, lambda: send("2b", SLOT[8], SLOT[2], k, tz2).start())
        when(z_minus & z_high, lambda: send("4a", SLOT[8], RELAY_Z, k, tzm2).start())

    def s1(k):
        arrive(SLOT[1], k)
        when(z < 7, lambda: send("2", SLOT[1], SLOT[2], k, t1).start())

    def s2(k):
        arrive(SLOT[2], k)
        when(z_plus, lambda: send("4", SLOT[2], SLOT[4], k, tz2).start())

    def sz(k):
        @pl.when(z_forward)
        def _():
            arrive(RELAY_Z, k)
            send("4f", RELAY_Z, SLOT[4], k, tzm2).start()

    def s128(k):
        arrive(SLOT[128], k)
        when(no(y_odd), lambda: send("256", SLOT[128], SLOT[256], k, y2).start())

    def sy(k):
        @pl.when(y_odd)
        def _():
            arrive(RELAY_Y, k)
            send("256", RELAY_Y, SLOT[256], k, ym2).start()

    stage = {"64": s64, "8": s8, "1": s1, "2": s2, "z": sz, "128": s128, "y": sy}
    depth = max(d for _, d in STAGES)

    q_copy.wait()
    scale = jnp.float32(FEATURES ** -0.5 * 1.4426950408889634)
    for b in range(2):
        for n in range(HEADS):
            part = q_vmem[b * BLOCK:(b + 1) * BLOCK, n * FEATURES:(n + 1) * FEATURES] * scale
            high, low = split(part)
            at = pl.ds((n % PER_GROUP) * BLOCK, BLOCK)
            q_cat[b, n // PER_GROUP, at, 0:FEATURES] = high
            q_cat[b, n // PER_GROUP, at, FEATURES:] = low
    acc[...] = jnp.zeros_like(acc)
    total[...] = jnp.zeros_like(total)
    top[...] = jnp.full_like(top, NEG)

    def relay(t, _):
        for name, d in STAGES:
            when((t >= d) & (t < CHUNKS + d), lambda name=name, d=d: stage[name](t - d))
        return 0

    lax.fori_loop(0, CHUNKS + depth, relay, 0)

    col = lax.broadcasted_iota(jnp.int32, (BLOCK, 256), 1)
    row = lax.broadcasted_iota(jnp.int32, (BLOCK, 256), 0)

    def wait_all(offsets):
        def body(k, _):
            for o in offsets:
                arrive(SLOT[o], k)
            return 0
        lax.fori_loop(0, CHUNKS, body, 0)

    def step(i, _):
        j, b = i // 2, i % 2
        when(i == 4, lambda: wait_all((16, 32)))
        when(i == 10, lambda: wait_all((4, 256)))
        where = []
        distance = []
        for p in range(2):
            o = pick(i, [STEPS[n % 2][n // 2][p][0] for n in range(12)])
            s = pick(i, [SLOT.get(STEPS[n % 2][n // 2][p][0], OWN) for n in range(12)])
            kb = pick(i, [STEPS[n % 2][n // 2][p][1] for n in range(12)])
            where.append((s, pl.ds(pl.multiple_of(kb * BLOCK, BLOCK), BLOCK)))
            distance.append(2 * o + b - kb)
        away = jnp.where(col < BLOCK, distance[0], distance[1])
        target = shard * 2 + b - away
        hit = target[0:8] == lists_ref[b, 0]
        for n in range(1, SLOTS):
            hit = hit | (target[0:8] == lists_ref[b, n])
        bias8 = jnp.where(hit & (target[0:8] >= 0), jnp.float32(0), jnp.float32(NEG))
        bias = jnp.where((away > 0) | (col % BLOCK <= row), jnp.broadcast_to(bias8[0:1], (BLOCK, 256)), jnp.float32(NEG))
        for n in range(GROUPS):
            keys = jnp.concatenate([buf[s, r, n * FEATURES:(n + 1) * FEATURES] for s, r in where], axis=0)
            values = jnp.concatenate([buf[s, r, 256 + n * FEATURES:256 + (n + 1) * FEATURES] for s, r in where], axis=0)
            k_high, k_low = split(keys)
            v_high, v_low = split(values)
            k_high = jnp.concatenate([k_high, k_high], axis=1)
            k_low = jnp.concatenate([k_low, k_low], axis=1)
            v_both = jnp.concatenate([v_high, v_low], axis=1)
            q = q_cat[b, n]
            dims = (((1,), (1,)), ((), ()))
            scores = lax.dot_general(q, k_high, dims, preferred_element_type=jnp.float32)
            scores = scores + lax.dot_general(q, k_low, dims, preferred_element_type=jnp.float32)
            scores = (scores.reshape(PER_GROUP, BLOCK, 256) + bias[None]).reshape(PER_GROUP * BLOCK, 256)
            old = top[b, n]
            new = jnp.maximum(old, jnp.max(scores, axis=1, keepdims=True))
            weights = jnp.exp2(scores - jnp.concatenate([new, new], axis=1))
            alpha = jnp.exp2(old - new)
            top[b, n] = new
            total[b, n] = total[b, n] * alpha + weights[:, :128] + weights[:, 128:]
            w_high, w_low = split(weights)
            o = jnp.dot(w_high, v_both, preferred_element_type=jnp.float32)
            o = o + jnp.dot(w_low, v_both, preferred_element_type=jnp.float32)
            acc[b, n] = acc[b, n] * alpha + o[:, :128] + o[:, 128:]
        return 0

    lax.fori_loop(0, 12, step, 0)

    for b in range(2):
        for n in range(GROUPS):
            out = acc[b, n] / jnp.sum(total[b, n], axis=1, keepdims=True)
            for r in range(PER_GROUP):
                m = n * PER_GROUP + r
                out_ref[b * BLOCK:(b + 1) * BLOCK, m * FEATURES:(m + 1) * FEATURES] = out[r * BLOCK:(r + 1) * BLOCK]

    def finish(k, _):
        def sent(rule):
            send(rule, OWN, SLOT[64], k, t1).wait_send()
        for rule in ("64", "8", "1", "32", "16", "128", "256"):
            sent(rule)
        when(z < 7, lambda: sent("2"))
        when(z == 6, lambda: sent("2b"))
        when(z_plus, lambda: sent("4"))
        when(z_forward, lambda: sent("4f"))
        when(z_minus, lambda: sent("4a"))
        when(y_odd, lambda: sent("256a"))
        return 0

    lax.fori_loop(0, CHUNKS, finish, 0)


def body(query_matrix, key_matrix, value_matrix, block_lists):
    pair = (2, GROUPS, PER_GROUP * BLOCK)
    return pl.pallas_call(
        kernel,
        out_shape=jax.ShapeDtypeStruct((ROWS, HEADS * FEATURES), jnp.float32),
        in_specs=[pl.BlockSpec(memory_space=pl.ANY)] * 3 + [pl.BlockSpec(memory_space=pltpu.SMEM)],
        out_specs=pl.BlockSpec(memory_space=pltpu.VMEM),
        scratch_shapes=[
            pltpu.VMEM((BUFFERS, ROWS, COLS), jnp.float32),
            pltpu.VMEM((ROWS, HEADS * FEATURES), jnp.float32),
            pltpu.VMEM(pair + (256,), jnp.bfloat16),
            pltpu.VMEM(pair + (FEATURES,), jnp.float32),
            pltpu.VMEM(pair + (128,), jnp.float32),
            pltpu.VMEM(pair + (128,), jnp.float32),
            pltpu.SemaphoreType.DMA((len(RULES), CHUNKS)),
            pltpu.SemaphoreType.DMA((BUFFERS, CHUNKS)),
            pltpu.SemaphoreType.DMA((3,)),
        ],
        compiler_params=pltpu.CompilerParams(collective_id=0, has_side_effects=True, vmem_limit_bytes=56 << 20),
    )(query_matrix, key_matrix, value_matrix, block_lists)


def solution(mesh):
    spec = P(("ctxhi", "ctxlo"), None)
    return jax.shard_map(body, mesh=mesh, in_specs=(spec,) * 4, out_specs=spec, check_vma=False)
```

```python
import jax
import jax.numpy as jnp
from jax import lax
from jax.experimental import pallas as pl
from jax.experimental.pallas import tpu as pltpu
from jax.sharding import PartitionSpec as P

HEADS, GROUPS, FEATURES, BLOCK = 12, 2, 128, 128
PER_GROUP = HEADS // GROUPS
SLOTS = 15
ROWS, COLS = 256, 512
OFFSETS = (1, 2, 4, 8, 16, 32, 64, 128, 256)
OWN = 0
SLOT = {o: i + 1 for i, o in enumerate(OFFSETS)}
RELAY_Z, RELAY_Y = 10, 11
BUFFERS = 12
RULES = ("1", "2", "2b", "4", "4f", "4a", "8", "16", "32", "64", "128", "256", "256a")
CHUNKS = 8
CHUNK = ROWS // CHUNKS
Z_BACK = (2, 6, 1, 6, 8, 8, 1, 6)
Y_BACK = 4
STAGES = (("8", 0), ("64", 0), ("1", 0), ("own 32", 4), ("32", 8), ("z", 8), ("y", 8), ("2", 8), ("128", 8))
TURNS = 28
WORK = {1: 0, 2: 1, 4: 2, 5: 3, **{t: t - 4 for t in range(8, TURNS)}}
NEG = -1e30
MESH = pl.DeviceIdType.MESH

STEPS = (
    (1, (0, 0), (0, 1)), (0, (0, 0), (8, 0)), (0, (1, 0), (1, 1)), (1, (1, 0), (1, 1)), (1, (8, 1), (64, 1)), (0, (64, 0), (128, 0)),
    (0, (2, 0), (2, 1)), (1, (2, 1), (128, 1)), (0, (32, 0), (16, 0)), (1, (32, 1), (16, 1)), (0, (4, 0), (256, 0)), (1, (4, 1), (256, 1)),
)


def pick(index, values):
    out = jnp.int32(values[0])
    for i, v in enumerate(values[1:], 1):
        if v != values[i - 1]:
            out = jnp.where(index >= i, jnp.int32(v), out)
    return out


def split(a):
    hi = a.astype(jnp.bfloat16)
    return hi, (a - hi.astype(jnp.float32)).astype(jnp.bfloat16)


def kernel(q_ref, k_ref, v_ref, lists_ref, out_ref, buf, q_vmem, q_cat, acc, top, total, ssem, rsem, lsem):
    lo, hi = lax.axis_index("ctxlo"), lax.axis_index("ctxhi")
    h, z = lo // 8, lo % 8
    y, g, c = hi // 4, (hi // 2) % 2, hi % 2
    x = h * 2 + g
    shard = hi * 16 + lo

    def dev(dy, dx, dz, core):
        xx = (x + dx + 4) % 4
        return {"ctxlo": (xx // 2) * 8 + (z + dz + 8) % 8, "ctxhi": ((y + dy + 8) % 8) * 4 + (xx % 2) * 2 + core}

    k_copy = pltpu.make_async_copy(k_ref, buf.at[OWN, :, pl.ds(0, 256)], lsem.at[0])
    v_copy = pltpu.make_async_copy(v_ref, buf.at[OWN, :, pl.ds(256, 256)], lsem.at[1])
    q_copy = pltpu.make_async_copy(q_ref, q_vmem, lsem.at[2])
    k_copy.start()
    v_copy.start()
    q_copy.start()
    barrier = pltpu.get_barrier_semaphore()
    f = 1 - c
    peers = [dev(0, 0, 1, c), dev(0, 0, -1, c), dev(0, 0, 2, c), dev(0, 0, -2, c), dev(1, 0, 0, c), dev(-1, 0, 0, c),
             dev(2, 0, 0, c), dev(-2, 0, 0, c), dev(0, 1, 0, c), dev(0, -1, 0, c), dev(0, 1, 0, f), dev(0, -1, 0, f),
             dev(0, 2, 0, c), dev(0, 2, 0, f), dev(0, 0, 0, f)]
    for peer in peers:
        pl.semaphore_signal(barrier, 1, device_id=peer, device_id_type=MESH)
    k_copy.wait()
    v_copy.wait()
    pl.semaphore_wait(barrier, len(peers))

    def rows(k):
        return pl.ds(pl.multiple_of(k * CHUNK, CHUNK), CHUNK)

    def send(rule, src, dst, k, target):
        return pltpu.make_async_remote_copy(
            src_ref=buf.at[src, rows(k)], dst_ref=buf.at[dst, rows(k)],
            send_sem=ssem.at[RULES.index(rule), k], recv_sem=rsem.at[dst, k],
            device_id=target, device_id_type=MESH)

    def arrive(dst, k):
        send("1", dst, dst, k, peers[0]).wait_recv()

    t1, tz2, tzm2 = peers[0], peers[2], peers[3]

    def z_back(away):
        return pick(z, [Z_BACK[(i + away) % 8] for i in range(8)])

    back_own, back_relay, back_plus = z_back(0), z_back(2), z_back(-2)
    y1, y2, ym2 = peers[4], peers[6], peers[7]
    side = jnp.where(g == 0, 1, -1)
    t32 = dev(0, side, 0, c)
    t16 = dev(0, 0, 0, f)
    top_x = h == 1
    carry = top_x & (c == 1)
    t8 = dev(0, jnp.where(carry, -side, 2), 0, jnp.where(top_x, f, c))
    g1 = g == 1
    y8 = g1 & carry
    z_high = z >= 4
    no = jnp.logical_not

    def when(condition, action):
        pl.when(condition)(action)

    def own(rule, dst, target, condition=None):
        def go(k):
            if condition is None:
                send(rule, OWN, dst, k, target).start()
            else:
                when(condition(k), lambda: send(rule, OWN, dst, k, target).start())
        return go

    own_32 = own("32", SLOT[32], t32, lambda k: no(g1))
    for go in (own("64", SLOT[64], y1), own("8", SLOT[8], t8, lambda k: no(y8)), own("1", SLOT[1], t1, lambda k: z < 7),
               own("4a", RELAY_Z, tzm2, lambda k: (k < back_own) & no(z_high)),
               own("16", SLOT[16], t16, lambda k: c == 0), own("256a", RELAY_Y, ym2, lambda k: k < Y_BACK)):
        def first(k, _, go=go):
            go(k)
            return 0
        lax.fori_loop(0, CHUNKS, first, 0)

    def s64(k):
        arrive(SLOT[64], k)
        send("128", SLOT[64], SLOT[128], k, y1).start()
        when(y8, lambda: send("8", SLOT[64], SLOT[8], k, t8).start())
        when(g1, lambda: send("32", SLOT[64], SLOT[32], k, t32).start())

    def s32(k):
        arrive(SLOT[32], k)
        when(c == 1, lambda: send("16", SLOT[32], SLOT[16], k, t16).start())

    def s8(k):
        arrive(SLOT[8], k)
        when(z == 6, lambda: send("2b", SLOT[8], SLOT[2], k, tz2).start())
        when(z == 7, lambda: send("1", SLOT[8], SLOT[1], k, t1).start())
        when((k < back_own) & z_high, lambda: send("4a", SLOT[8], RELAY_Z, k, tzm2).start())

    def s1(k):
        arrive(SLOT[1], k)
        when(z < 7, lambda: send("2", SLOT[1], SLOT[2], k, t1).start())

    def s2(k):
        arrive(SLOT[2], k)
        when(k >= back_plus, lambda: send("4", SLOT[2], SLOT[4], k, tz2).start())

    def sz(k):
        @pl.when(k < back_relay)
        def _():
            arrive(RELAY_Z, k)
            send("4f", RELAY_Z, SLOT[4], k, tzm2).start()

    def s128(k):
        arrive(SLOT[128], k)
        when(k >= Y_BACK, lambda: send("256", SLOT[128], SLOT[256], k, y2).start())

    def sy(k):
        @pl.when(k < Y_BACK)
        def _():
            arrive(RELAY_Y, k)
            send("256", RELAY_Y, SLOT[256], k, ym2).start()

    stage = {"64": s64, "8": s8, "1": s1, "2": s2, "z": sz, "128": s128, "y": sy, "32": s32, "own 32": own_32}

    q_copy.wait()
    scale = jnp.float32(FEATURES ** -0.5 * 1.4426950408889634)
    for b in range(2):
        for n in range(HEADS):
            part = q_vmem[b * BLOCK:(b + 1) * BLOCK, n * FEATURES:(n + 1) * FEATURES] * scale
            high, low = split(part)
            at = pl.ds((n % PER_GROUP) * BLOCK, BLOCK)
            q_cat[b, n // PER_GROUP, at, 0:FEATURES] = high
            q_cat[b, n // PER_GROUP, at, FEATURES:] = low
    acc[...] = jnp.zeros_like(acc)
    total[...] = jnp.zeros_like(total)
    top[...] = jnp.full_like(top, NEG)

    col = lax.broadcasted_iota(jnp.int32, (BLOCK, 256), 1)
    row = lax.broadcasted_iota(jnp.int32, (BLOCK, 256), 0)

    def wait_all(offsets):
        def body(k, _):
            for o in offsets:
                arrive(SLOT[o], k)
            return 0
        lax.fori_loop(0, CHUNKS, body, 0)

    def step(i, n):
        b = pick(i, [s[0] for s in STEPS])
        where = []
        distance = []
        for p in (1, 2):
            o = pick(i, [s[p][0] for s in STEPS])
            slot = pick(i, [SLOT.get(s[p][0], OWN) for s in STEPS])
            kb = pick(i, [s[p][1] for s in STEPS])
            where.append((slot, pl.ds(pl.multiple_of(kb * BLOCK, BLOCK), BLOCK)))
            distance.append(2 * o + b - kb)
        away = jnp.where(col < BLOCK, distance[0], distance[1])
        target = shard * 2 + b - away
        hit = target[0:8] == lists_ref[b, 0]
        for m in range(1, SLOTS):
            hit = hit | (target[0:8] == lists_ref[b, m])
        bias8 = jnp.where(hit & (target[0:8] >= 0), jnp.float32(0), jnp.float32(NEG))
        bias = jnp.where((away > 0) | (col % BLOCK <= row), jnp.broadcast_to(bias8[0:1], (BLOCK, 256)), jnp.float32(NEG))
        def lanes(start):
            return pl.ds(pl.multiple_of(start + n * FEATURES, FEATURES), FEATURES)

        keys = jnp.concatenate([buf[s, r, lanes(0)] for s, r in where], axis=0)
        values = jnp.concatenate([buf[s, r, lanes(256)] for s, r in where], axis=0)
        k_high, k_low = split(keys)
        v_high, v_low = split(values)
        k_high = jnp.concatenate([k_high, k_high], axis=1)
        k_low = jnp.concatenate([k_low, k_low], axis=1)
        v_both = jnp.concatenate([v_high, v_low], axis=1)
        q = q_cat[b, n]
        dims = (((1,), (1,)), ((), ()))
        scores = lax.dot_general(q, k_high, dims, preferred_element_type=jnp.float32)
        scores = scores + lax.dot_general(q, k_low, dims, preferred_element_type=jnp.float32)
        scores = (scores.reshape(PER_GROUP, BLOCK, 256) + bias[None]).reshape(PER_GROUP * BLOCK, 256)
        old = top[b, n]
        new = jnp.maximum(old, jnp.max(scores, axis=1, keepdims=True))
        weights = jnp.exp2(scores - jnp.concatenate([new, new], axis=1))
        alpha = jnp.exp2(old - new)
        top[b, n] = new
        total[b, n] = total[b, n] * alpha + weights[:, :128] + weights[:, 128:]
        w_high, w_low = split(weights)
        o = jnp.dot(w_high, v_both, preferred_element_type=jnp.float32)
        o = o + jnp.dot(w_low, v_both, preferred_element_type=jnp.float32)
        acc[b, n] = acc[b, n] * alpha + o[:, :128] + o[:, 128:]

    def turn(t, _):
        for name, start in STAGES:
            when((t >= start) & (t < start + CHUNKS), lambda name=name, start=start: stage[name](t - start))
        when(t == 20, lambda: wait_all((16,)))
        when(t == 24, lambda: wait_all((4, 256)))
        half = pick(t, [WORK.get(i, -1) for i in range(TURNS)])

        @pl.when(half >= 0)
        def _():
            step(half // 2, half % 2)
        return 0

    lax.fori_loop(0, TURNS, turn, 0)

    for b in range(2):
        for n in range(GROUPS):
            out = acc[b, n] / jnp.sum(total[b, n], axis=1, keepdims=True)
            for r in range(PER_GROUP):
                m = n * PER_GROUP + r
                out_ref[b * BLOCK:(b + 1) * BLOCK, m * FEATURES:(m + 1) * FEATURES] = out[r * BLOCK:(r + 1) * BLOCK]

    def finish(k, _):
        def sent(rule):
            send(rule, OWN, SLOT[64], k, t1).wait_send()
        for rule in ("64", "8", "1", "32", "16", "128", "256"):
            sent(rule)
        when(z < 7, lambda: sent("2"))
        when(z == 6, lambda: sent("2b"))
        when(k >= back_plus, lambda: sent("4"))
        when(k < back_relay, lambda: sent("4f"))
        when(k < back_own, lambda: sent("4a"))
        when(k < Y_BACK, lambda: sent("256a"))
        return 0

    lax.fori_loop(0, CHUNKS, finish, 0)


def body(query_matrix, key_matrix, value_matrix, block_lists):
    pair = (2, GROUPS, PER_GROUP * BLOCK)
    return pl.pallas_call(
        kernel,
        out_shape=jax.ShapeDtypeStruct((ROWS, HEADS * FEATURES), jnp.float32),
        in_specs=[pl.BlockSpec(memory_space=pl.ANY)] * 3 + [pl.BlockSpec(memory_space=pltpu.SMEM)],
        out_specs=pl.BlockSpec(memory_space=pltpu.VMEM),
        scratch_shapes=[
            pltpu.VMEM((BUFFERS, ROWS, COLS), jnp.float32),
            pltpu.VMEM((ROWS, HEADS * FEATURES), jnp.float32),
            pltpu.VMEM(pair + (256,), jnp.bfloat16),
            pltpu.VMEM(pair + (FEATURES,), jnp.float32),
            pltpu.VMEM(pair + (128,), jnp.float32),
            pltpu.VMEM(pair + (128,), jnp.float32),
            pltpu.SemaphoreType.DMA((len(RULES), CHUNKS)),
            pltpu.SemaphoreType.DMA((BUFFERS, CHUNKS)),
            pltpu.SemaphoreType.DMA((3,)),
        ],
        compiler_params=pltpu.CompilerParams(collective_id=0, has_side_effects=True, vmem_limit_bytes=56 << 20),
    )(query_matrix, key_matrix, value_matrix, block_lists)


def solution(mesh):
    spec = P(("ctxhi", "ctxlo"), None)
    return jax.shard_map(body, mesh=mesh, in_specs=(spec,) * 4, out_specs=spec, check_vma=False)
```

```python
import jax
import jax.numpy as jnp
from jax import lax
from jax.experimental import pallas as pl
from jax.experimental.pallas import tpu as pltpu
from jax.sharding import PartitionSpec as P

HEADS, GROUPS, FEATURES, BLOCK = 12, 2, 128, 128
PER_GROUP = HEADS // GROUPS
SLOTS = 15
ROWS, COLS = 256, 512
OFFSETS = (1, 2, 4, 8, 16, 32, 64, 128, 256)
OWN = 0
SLOT = {o: i + 1 for i, o in enumerate(OFFSETS)}
RELAY_Z, RELAY_Y = 10, 11
BUFFERS = 12
RULES = ("1", "2", "2b", "4", "4f", "4a", "8", "16", "32", "64", "128", "256", "256a")
CHUNKS = 8
CHUNK = ROWS // CHUNKS
Z_BACK = (2, 6, 1, 6, 8, 8, 1, 6)
Y_BACK = 4
STAGES = (("8", 0), ("64", 0), ("1", 0), ("own 32", 4), ("32", 8), ("z", 8), ("y", 8), ("2", 8), ("128", 8))
TURNS = 25
WORK = {t: t - 1 for t in range(1, TURNS)}
NEG = -1e30
MESH = pl.DeviceIdType.MESH

STEPS = (
    (1, (0, 0), (0, 1)), (0, (0, 0), (8, 0)), (0, (1, 0), (64, 0)), (1, (1, 0), (1, 1)), (1, (8, 1), (64, 1)), (0, (1, 1), (128, 0)),
    (0, (2, 0), (32, 0)), (1, (2, 1), (128, 1)), (0, (2, 1), (16, 0)), (1, (32, 1), (16, 1)), (0, (4, 0), (256, 0)), (1, (4, 1), (256, 1)),
)


def pick(index, values):
    out = jnp.int32(values[0])
    for i, v in enumerate(values[1:], 1):
        if v != values[i - 1]:
            out = jnp.where(index >= i, jnp.int32(v), out)
    return out


def split(a):
    hi = a.astype(jnp.bfloat16)
    return hi, (a - hi.astype(jnp.float32)).astype(jnp.bfloat16)


def kernel(q_ref, k_ref, v_ref, lists_ref, out_ref, buf, q_vmem, q_cat, acc, top, total, ssem, rsem, lsem):
    lo, hi = lax.axis_index("ctxlo"), lax.axis_index("ctxhi")
    h, z = lo // 8, lo % 8
    y, g, c = hi // 4, (hi // 2) % 2, hi % 2
    x = h * 2 + g
    shard = hi * 16 + lo

    def dev(dy, dx, dz, core):
        xx = (x + dx + 4) % 4
        return {"ctxlo": (xx // 2) * 8 + (z + dz + 8) % 8, "ctxhi": ((y + dy + 8) % 8) * 4 + (xx % 2) * 2 + core}

    k_copy = pltpu.make_async_copy(k_ref, buf.at[OWN, :, pl.ds(0, 256)], lsem.at[0])
    v_copy = pltpu.make_async_copy(v_ref, buf.at[OWN, :, pl.ds(256, 256)], lsem.at[1])
    q_copy = pltpu.make_async_copy(q_ref, q_vmem, lsem.at[2])
    k_copy.start()
    v_copy.start()
    q_copy.start()
    barrier = pltpu.get_barrier_semaphore()
    f = 1 - c
    peers = [dev(0, 0, 1, c), dev(0, 0, -1, c), dev(0, 0, 2, c), dev(0, 0, -2, c), dev(1, 0, 0, c), dev(-1, 0, 0, c),
             dev(2, 0, 0, c), dev(-2, 0, 0, c), dev(0, 1, 0, c), dev(0, -1, 0, c), dev(0, 1, 0, f), dev(0, -1, 0, f),
             dev(0, 2, 0, c), dev(0, 2, 0, f), dev(0, 0, 0, f)]
    for peer in peers:
        pl.semaphore_signal(barrier, 1, device_id=peer, device_id_type=MESH)
    k_copy.wait()
    v_copy.wait()
    pl.semaphore_wait(barrier, len(peers))

    def rows(k):
        return pl.ds(pl.multiple_of(k * CHUNK, CHUNK), CHUNK)

    def send(rule, src, dst, k, target):
        return pltpu.make_async_remote_copy(
            src_ref=buf.at[src, rows(k)], dst_ref=buf.at[dst, rows(k)],
            send_sem=ssem.at[RULES.index(rule), k], recv_sem=rsem.at[dst, k],
            device_id=target, device_id_type=MESH)

    def arrive(dst, k):
        send("1", dst, dst, k, peers[0]).wait_recv()

    t1, tz2, tzm2 = peers[0], peers[2], peers[3]

    def z_back(away):
        return pick(z, [Z_BACK[(i + away) % 8] for i in range(8)])

    back_own, back_relay, back_plus = z_back(0), z_back(2), z_back(-2)
    y1, y2, ym2 = peers[4], peers[6], peers[7]
    side = jnp.where(g == 0, 1, -1)
    t32 = dev(0, side, 0, c)
    t16 = dev(0, 0, 0, f)
    top_x = h == 1
    carry = top_x & (c == 1)
    t8 = dev(0, jnp.where(carry, -side, 2), 0, jnp.where(top_x, f, c))
    g1 = g == 1
    y8 = g1 & carry
    z_high = z >= 4
    no = jnp.logical_not

    def when(condition, action):
        pl.when(condition)(action)

    def own(rule, dst, target, condition=None):
        def go(k):
            if condition is None:
                send(rule, OWN, dst, k, target).start()
            else:
                when(condition(k), lambda: send(rule, OWN, dst, k, target).start())
        return go

    own_32 = own("32", SLOT[32], t32, lambda k: no(g1))
    for go in (own("64", SLOT[64], y1), own("8", SLOT[8], t8, lambda k: no(y8)), own("1", SLOT[1], t1, lambda k: z < 7),
               own("4a", RELAY_Z, tzm2, lambda k: (k < back_own) & no(z_high)),
               own("16", SLOT[16], t16, lambda k: c == 0), own("256a", RELAY_Y, ym2, lambda k: k < Y_BACK)):
        def first(k, _, go=go):
            go(k)
            return 0
        lax.fori_loop(0, CHUNKS, first, 0)

    def s64(k):
        arrive(SLOT[64], k)
        send("128", SLOT[64], SLOT[128], k, y1).start()
        when(y8, lambda: send("8", SLOT[64], SLOT[8], k, t8).start())
        when(g1, lambda: send("32", SLOT[64], SLOT[32], k, t32).start())

    def s32(k):
        arrive(SLOT[32], k)
        when(c == 1, lambda: send("16", SLOT[32], SLOT[16], k, t16).start())

    def s8(k):
        arrive(SLOT[8], k)
        when(z == 6, lambda: send("2b", SLOT[8], SLOT[2], k, tz2).start())
        when(z == 7, lambda: send("1", SLOT[8], SLOT[1], k, t1).start())
        when((k < back_own) & z_high, lambda: send("4a", SLOT[8], RELAY_Z, k, tzm2).start())

    def s1(k):
        arrive(SLOT[1], k)
        when(z < 7, lambda: send("2", SLOT[1], SLOT[2], k, t1).start())

    def s2(k):
        arrive(SLOT[2], k)
        when(k >= back_plus, lambda: send("4", SLOT[2], SLOT[4], k, tz2).start())

    def sz(k):
        @pl.when(k < back_relay)
        def _():
            arrive(RELAY_Z, k)
            send("4f", RELAY_Z, SLOT[4], k, tzm2).start()

    def s128(k):
        arrive(SLOT[128], k)
        when(k >= Y_BACK, lambda: send("256", SLOT[128], SLOT[256], k, y2).start())

    def sy(k):
        @pl.when(k < Y_BACK)
        def _():
            arrive(RELAY_Y, k)
            send("256", RELAY_Y, SLOT[256], k, ym2).start()

    stage = {"64": s64, "8": s8, "1": s1, "2": s2, "z": sz, "128": s128, "y": sy, "32": s32, "own 32": own_32}

    q_copy.wait()
    scale = jnp.float32(FEATURES ** -0.5 * 1.4426950408889634)
    for b in range(2):
        for n in range(HEADS):
            part = q_vmem[b * BLOCK:(b + 1) * BLOCK, n * FEATURES:(n + 1) * FEATURES] * scale
            high, low = split(part)
            at = pl.ds((n % PER_GROUP) * BLOCK, BLOCK)
            q_cat[b, n // PER_GROUP, at, 0:FEATURES] = high
            q_cat[b, n // PER_GROUP, at, FEATURES:] = low
    acc[...] = jnp.zeros_like(acc)
    total[...] = jnp.zeros_like(total)
    top[...] = jnp.full_like(top, NEG)

    col = lax.broadcasted_iota(jnp.int32, (BLOCK, 256), 1)
    row = lax.broadcasted_iota(jnp.int32, (BLOCK, 256), 0)

    def wait_all(offsets, start=0, stop=CHUNKS):
        def body(k, _):
            for o in offsets:
                arrive(SLOT[o], k)
            return 0
        lax.fori_loop(start, stop, body, 0)

    def step(i, n):
        b = pick(i, [s[0] for s in STEPS])
        where = []
        distance = []
        for p in (1, 2):
            o = pick(i, [s[p][0] for s in STEPS])
            slot = pick(i, [SLOT.get(s[p][0], OWN) for s in STEPS])
            kb = pick(i, [s[p][1] for s in STEPS])
            where.append((slot, pl.ds(pl.multiple_of(kb * BLOCK, BLOCK), BLOCK)))
            distance.append(2 * o + b - kb)
        away = jnp.where(col < BLOCK, distance[0], distance[1])
        target = shard * 2 + b - away
        hit = target[0:8] == lists_ref[b, 0]
        for m in range(1, SLOTS):
            hit = hit | (target[0:8] == lists_ref[b, m])
        bias8 = jnp.where(hit & (target[0:8] >= 0), jnp.float32(0), jnp.float32(NEG))
        bias = jnp.where((away > 0) | (col % BLOCK <= row), jnp.broadcast_to(bias8[0:1], (BLOCK, 256)), jnp.float32(NEG))

        def lanes(start):
            return pl.ds(pl.multiple_of(start + n * FEATURES, FEATURES), FEATURES)

        keys = jnp.concatenate([buf[s, r, lanes(0)] for s, r in where], axis=0)
        values = jnp.concatenate([buf[s, r, lanes(256)] for s, r in where], axis=0)
        k_high, k_low = split(keys)
        v_high, v_low = split(values)
        k_cat = jnp.concatenate([k_high, k_high, k_low, k_low], axis=1)
        v_both = jnp.concatenate([v_high, v_low], axis=1)
        v_cat = jnp.concatenate([v_both, v_both], axis=0)
        dims = (((1,), (1,)), ((), ()))
        q = q_cat[b, n]
        scores = lax.dot_general(jnp.concatenate([q, q], axis=1), k_cat, dims, preferred_element_type=jnp.float32)
        scores = (scores.reshape(PER_GROUP, BLOCK, 256) + bias[None]).reshape(PER_GROUP * BLOCK, 256)
        old = top[b, n]
        new = jnp.maximum(old, jnp.max(scores, axis=1, keepdims=True))
        weights = jnp.exp2(scores - jnp.concatenate([new, new], axis=1))
        alpha = jnp.exp2(old - new)
        top[b, n] = new
        total[b, n] = total[b, n] * alpha + weights[:, :128] + weights[:, 128:]
        w_high, w_low = split(weights)
        o = jnp.dot(jnp.concatenate([w_high, w_low], axis=1), v_cat, preferred_element_type=jnp.float32)
        acc[b, n] = acc[b, n] * alpha + o[:, :128] + o[:, 128:]

    def turn(t, _):
        for name, start in STAGES:
            when((t >= start) & (t < start + CHUNKS), lambda name=name, start=start: stage[name](t - start))
        when(t == 17, lambda: wait_all((16,)))
        when(t == 21, lambda: wait_all((4, 256), 0, CHUNKS // 2))
        when(t == 23, lambda: wait_all((4, 256), CHUNKS // 2))
        half = pick(t, [WORK.get(i, -1) for i in range(TURNS)])

        @pl.when(half >= 0)
        def _():
            step(half // 2, half % 2)
        return 0

    lax.fori_loop(0, TURNS, turn, 0)

    for b in range(2):
        for n in range(GROUPS):
            out = acc[b, n] * (1 / jnp.sum(total[b, n], axis=1, keepdims=True))
            for r in range(PER_GROUP):
                m = n * PER_GROUP + r
                out_ref[b * BLOCK:(b + 1) * BLOCK, m * FEATURES:(m + 1) * FEATURES] = out[r * BLOCK:(r + 1) * BLOCK]

    def finish(k, _):
        def sent(rule):
            send(rule, OWN, SLOT[64], k, t1).wait_send()
        for rule in ("64", "8", "1", "32", "16", "128", "256"):
            sent(rule)
        when(z < 7, lambda: sent("2"))
        when(z == 6, lambda: sent("2b"))
        when(k >= back_plus, lambda: sent("4"))
        when(k < back_relay, lambda: sent("4f"))
        when(k < back_own, lambda: sent("4a"))
        when(k < Y_BACK, lambda: sent("256a"))
        return 0

    lax.fori_loop(0, CHUNKS, finish, 0)


def body(query_matrix, key_matrix, value_matrix, block_lists):
    pair = (2, GROUPS, PER_GROUP * BLOCK)
    return pl.pallas_call(
        kernel,
        out_shape=pltpu.VMEM((ROWS, HEADS * FEATURES), jnp.float32),
        in_specs=[pl.BlockSpec(memory_space=pl.ANY)] * 3 + [pl.BlockSpec(memory_space=pltpu.SMEM)],
        out_specs=pl.BlockSpec(memory_space=pltpu.VMEM),
        scratch_shapes=[
            pltpu.VMEM((BUFFERS, ROWS, COLS), jnp.float32),
            pltpu.VMEM((ROWS, HEADS * FEATURES), jnp.float32),
            pltpu.VMEM(pair + (256,), jnp.bfloat16),
            pltpu.VMEM(pair + (FEATURES,), jnp.float32),
            pltpu.VMEM(pair + (128,), jnp.float32),
            pltpu.VMEM(pair + (128,), jnp.float32),
            pltpu.SemaphoreType.DMA((len(RULES), CHUNKS)),
            pltpu.SemaphoreType.DMA((BUFFERS, CHUNKS)),
            pltpu.SemaphoreType.DMA((3,)),
        ],
        compiler_params=pltpu.CompilerParams(collective_id=0, has_side_effects=True, vmem_limit_bytes=56 << 20),
    )(query_matrix, key_matrix, value_matrix, block_lists)


def solution(mesh):
    spec = P(("ctxhi", "ctxlo"), None)
    return jax.shard_map(body, mesh=mesh, in_specs=(spec,) * 4, out_specs=spec, check_vma=False)
```

```python
import jax
import jax.numpy as jnp
from jax import lax
from jax.experimental import pallas as pl
from jax.experimental.pallas import tpu as pltpu
from jax.sharding import PartitionSpec as P

HEADS, GROUPS, FEATURES, BLOCK = 12, 2, 128, 128
PER_GROUP = HEADS // GROUPS
SLOTS = 15
ROWS, COLS = 256, 512
OFFSETS = (1, 2, 4, 8, 16, 32, 64, 128, 256)
OWN = 0
SLOT = {o: i + 1 for i, o in enumerate(OFFSETS)}
RELAY_Z, RELAY_Y = 10, 11
BUFFERS = 12
RULES = ("1", "2", "2b", "4", "4f", "4a", "8", "16", "32", "64", "128", "256", "256a")
CHUNKS = 8
CHUNK = ROWS // CHUNKS
Z_BACK = (4, 6, 2, 8, 8, 8, 2, 6)
Y_BACK = 5
STAGES = (("8", 0), ("64", 0), ("1", 0), ("own 32", 1), ("32", 8), ("y", 8), ("128", 8), ("z", 8), ("2", 8))
TURNS = 21
WORK = {2: 0, 4: 1, 6: 2, 8: 3, 10: 4, 12: 5, 14: 6, **{t: t - 9 for t in range(16, TURNS)}}
NEG = -1e30
MESH = pl.DeviceIdType.MESH

STEPS = (
    (1, (0, 0), (0, 1)), (0, (0, 0), (8, 0)), (0, (1, 0), (64, 0)), (1, (1, 0), (1, 1)), (1, (8, 1), (64, 1)), (0, (1, 1), (128, 0)),
    (0, (2, 0), (32, 0)), (1, (2, 1), (128, 1)), (0, (2, 1), (16, 0)), (1, (32, 1), (16, 1)), (0, (4, 0), (256, 0)), (1, (4, 1), (256, 1)),
)


def pick(index, values):
    out = jnp.int32(values[0])
    for i, v in enumerate(values[1:], 1):
        if v != values[i - 1]:
            out = jnp.where(index >= i, jnp.int32(v), out)
    return out


def split(a):
    hi = a.astype(jnp.bfloat16)
    return hi, (a - hi.astype(jnp.float32)).astype(jnp.bfloat16)


def kernel(q_ref, k_ref, v_ref, lists_ref, out_ref, buf, q_vmem, q_cat, acc, top, total, ssem, rsem, lsem):
    lo, hi = lax.axis_index("ctxlo"), lax.axis_index("ctxhi")
    h, z = lo // 8, lo % 8
    y, g, c = hi // 4, (hi // 2) % 2, hi % 2
    x = h * 2 + g
    shard = hi * 16 + lo

    def dev(dy, dx, dz, core):
        xx = (x + dx + 4) % 4
        return {"ctxlo": (xx // 2) * 8 + (z + dz + 8) % 8, "ctxhi": ((y + dy + 8) % 8) * 4 + (xx % 2) * 2 + core}

    k_copy = pltpu.make_async_copy(k_ref, buf.at[OWN, :, pl.ds(0, 256)], lsem.at[0])
    v_copy = pltpu.make_async_copy(v_ref, buf.at[OWN, :, pl.ds(256, 256)], lsem.at[1])
    q_copy = pltpu.make_async_copy(q_ref, q_vmem, lsem.at[2])
    k_copy.start()
    v_copy.start()
    q_copy.start()
    barrier = pltpu.get_barrier_semaphore()
    f = 1 - c
    peers = [dev(0, 0, 1, c), dev(0, 0, -1, c), dev(0, 0, 2, c), dev(0, 0, -2, c), dev(1, 0, 0, c), dev(-1, 0, 0, c),
             dev(2, 0, 0, c), dev(-2, 0, 0, c), dev(0, 1, 0, c), dev(0, -1, 0, c), dev(0, 1, 0, f), dev(0, -1, 0, f),
             dev(0, 2, 0, c), dev(0, 2, 0, f), dev(0, 0, 0, f)]
    for peer in peers:
        pl.semaphore_signal(barrier, 1, device_id=peer, device_id_type=MESH)
    k_copy.wait()
    v_copy.wait()
    pl.semaphore_wait(barrier, len(peers))

    def rows(k):
        return pl.ds(pl.multiple_of(k * CHUNK, CHUNK), CHUNK)

    def send(rule, src, dst, k, target):
        return pltpu.make_async_remote_copy(
            src_ref=buf.at[src, rows(k)], dst_ref=buf.at[dst, rows(k)],
            send_sem=ssem.at[RULES.index(rule), k], recv_sem=rsem.at[dst, k],
            device_id=target, device_id_type=MESH)

    def arrive(dst, k):
        send("1", dst, dst, k, peers[0]).wait_recv()

    t1, tz2, tzm2 = peers[0], peers[2], peers[3]

    def z_back(away):
        return pick(z, [Z_BACK[(i + away) % 8] for i in range(8)])

    back_own, back_relay, back_plus = z_back(0), z_back(2), z_back(-2)
    y1, y2, ym2 = peers[4], peers[6], peers[7]
    side = jnp.where(g == 0, 1, -1)
    t32 = dev(0, side, 0, c)
    t16 = dev(0, 0, 0, f)
    top_x = h == 1
    carry = top_x & (c == 1)
    t8 = dev(0, jnp.where(carry, -side, 2), 0, jnp.where(top_x, f, c))
    g1 = g == 1
    y8 = g1 & carry
    z_high = z >= 4
    no = jnp.logical_not

    def when(condition, action):
        pl.when(condition)(action)

    def own(rule, dst, target, condition=None):
        def go(k):
            if condition is None:
                send(rule, OWN, dst, k, target).start()
            else:
                when(condition(k), lambda: send(rule, OWN, dst, k, target).start())
        return go

    own_32 = own("32", SLOT[32], t32, lambda k: no(g1))
    for go in (own("1", SLOT[1], t1, lambda k: z < 7), own("4a", RELAY_Z, tzm2, lambda k: (k < back_own) & no(z_high)),
               own("8", SLOT[8], t8, lambda k: no(y8)), own("64", SLOT[64], y1),
               own("16", SLOT[16], t16, lambda k: c == 0), own("256a", RELAY_Y, ym2, lambda k: k < Y_BACK)):
        def first(k, _, go=go):
            go(k)
            return 0
        lax.fori_loop(0, CHUNKS, first, 0)

    def s64(k):
        arrive(SLOT[64], k)
        send("128", SLOT[64], SLOT[128], k, y1).start()
        when(y8, lambda: send("8", SLOT[64], SLOT[8], k, t8).start())
        when(g1, lambda: send("32", SLOT[64], SLOT[32], k, t32).start())

    def s32(k):
        arrive(SLOT[32], k)
        when(c == 1, lambda: send("16", SLOT[32], SLOT[16], k, t16).start())

    def s8(k):
        arrive(SLOT[8], k)
        when(z == 6, lambda: send("2b", SLOT[8], SLOT[2], k, tz2).start())
        when(z == 7, lambda: send("1", SLOT[8], SLOT[1], k, t1).start())
        when((k < back_own) & z_high, lambda: send("4a", SLOT[8], RELAY_Z, k, tzm2).start())

    def s1(k):
        arrive(SLOT[1], k)
        when(z < 7, lambda: send("2", SLOT[1], SLOT[2], k, t1).start())

    def s2(k):
        arrive(SLOT[2], k)
        when(k >= back_plus, lambda: send("4", SLOT[2], SLOT[4], k, tz2).start())

    def sz(k):
        @pl.when(k < back_relay)
        def _():
            arrive(RELAY_Z, k)
            send("4f", RELAY_Z, SLOT[4], k, tzm2).start()

    def s128(k):
        arrive(SLOT[128], k)
        when(k >= Y_BACK, lambda: send("256", SLOT[128], SLOT[256], k, y2).start())

    def sy(k):
        @pl.when(k < Y_BACK)
        def _():
            arrive(RELAY_Y, k)
            send("256", RELAY_Y, SLOT[256], k, ym2).start()

    stage = {"64": s64, "8": s8, "1": s1, "2": s2, "z": sz, "128": s128, "y": sy, "32": s32, "own 32": own_32}

    q_copy.wait()
    scale = jnp.float32(FEATURES ** -0.5 * 1.4426950408889634)
    for b in range(2):
        for n in range(HEADS):
            part = q_vmem[b * BLOCK:(b + 1) * BLOCK, n * FEATURES:(n + 1) * FEATURES] * scale
            high, low = split(part)
            at = pl.ds((n % PER_GROUP) * BLOCK, BLOCK)
            q_cat[b, n // PER_GROUP, at, 0:FEATURES] = high
            q_cat[b, n // PER_GROUP, at, FEATURES:] = low
    acc[...] = jnp.zeros_like(acc)
    total[...] = jnp.zeros_like(total)
    top[...] = jnp.full_like(top, NEG)

    col = lax.broadcasted_iota(jnp.int32, (BLOCK, 256), 1)
    row = lax.broadcasted_iota(jnp.int32, (BLOCK, 256), 0)

    def wait_all(offsets, start=0, stop=CHUNKS):
        def body(k, _):
            for o in offsets:
                arrive(SLOT[o], k)
            return 0
        lax.fori_loop(start, stop, body, 0)

    def step(i):
        b = pick(i, [s[0] for s in STEPS])
        where = []
        distance = []
        for p in (1, 2):
            o = pick(i, [s[p][0] for s in STEPS])
            slot = pick(i, [SLOT.get(s[p][0], OWN) for s in STEPS])
            kb = pick(i, [s[p][1] for s in STEPS])
            where.append((slot, pl.ds(pl.multiple_of(kb * BLOCK, BLOCK), BLOCK)))
            distance.append(2 * o + b - kb)
        away = jnp.where(col < BLOCK, distance[0], distance[1])
        target = shard * 2 + b - away
        hit = target[0:8] == lists_ref[b, 0]
        for m in range(1, SLOTS):
            hit = hit | (target[0:8] == lists_ref[b, m])
        bias8 = jnp.where(hit & (target[0:8] >= 0), jnp.float32(0), jnp.float32(NEG))
        bias = jnp.where((away > 0) | (col % BLOCK <= row), jnp.broadcast_to(bias8[0:1], (BLOCK, 256)), jnp.float32(NEG))

        ahead = []
        for n in range(GROUPS):
            def lanes(start, n=n):
                return pl.ds(start + n * FEATURES, FEATURES)

            keys = jnp.concatenate([buf[s, r, lanes(0)] for s, r in where], axis=0)
            values = jnp.concatenate([buf[s, r, lanes(256)] for s, r in where], axis=0)
            k_high, k_low = split(keys)
            v_high, v_low = split(values)
            k_cat = jnp.concatenate([k_high, k_high, k_low, k_low], axis=1)
            v_both = jnp.concatenate([v_high, v_low], axis=1)
            v_cat = jnp.concatenate([v_both, v_both], axis=0)
            dims = (((1,), (1,)), ((), ()))
            q = q_cat[b, n]
            scores = lax.dot_general(jnp.concatenate([q, q], axis=1), k_cat, dims, preferred_element_type=jnp.float32)
            scores = (scores.reshape(PER_GROUP, BLOCK, 256) + bias[None]).reshape(PER_GROUP * BLOCK, 256)
            ahead.append((scores, v_cat))
        for n, (scores, v_cat) in enumerate(ahead):
            old = top[b, n]
            new = jnp.maximum(old, jnp.max(scores, axis=1, keepdims=True))
            weights = jnp.exp2(scores - jnp.concatenate([new, new], axis=1))
            alpha = jnp.exp2(old - new)
            top[b, n] = new
            total[b, n] = total[b, n] * alpha + weights[:, :128] + weights[:, 128:]
            w_high, w_low = split(weights)
            o = jnp.dot(jnp.concatenate([w_high, w_low], axis=1), v_cat, preferred_element_type=jnp.float32)
            acc[b, n] = acc[b, n] * alpha + o[:, :128] + o[:, 128:]

    def finish(k, _):
        def sent(rule):
            send(rule, OWN, SLOT[64], k, t1).wait_send()
        for rule in ("64", "8", "1", "32", "16", "128", "256"):
            sent(rule)
        when(z < 7, lambda: sent("2"))
        when(z == 6, lambda: sent("2b"))
        when(k >= back_plus, lambda: sent("4"))
        when(k < back_relay, lambda: sent("4f"))
        when(k < back_own, lambda: sent("4a"))
        when(k < Y_BACK, lambda: sent("256a"))
        return 0

    def turn(t, _):
        for name, start in STAGES:
            when((t >= start) & (t < start + CHUNKS), lambda name=name, start=start: stage[name](t - start))
        when(t == 17, lambda: wait_all((16,)))
        when(t == 19, lambda: wait_all((4, 256), 0, CHUNKS // 2))

        @pl.when(t == 20)
        def _():
            lax.fori_loop(0, CHUNKS, finish, 0)
            wait_all((4, 256), CHUNKS // 2)

        half = pick(t, [WORK.get(i, -1) for i in range(TURNS)])

        @pl.when(half >= 0)
        def _():
            step(half)
        return 0

    lax.fori_loop(0, TURNS, turn, 0)

    for b in range(2):
        for n in range(GROUPS):
            out = acc[b, n] * (1 / jnp.sum(total[b, n], axis=1, keepdims=True))
            for r in range(PER_GROUP):
                m = n * PER_GROUP + r
                out_ref[b * BLOCK:(b + 1) * BLOCK, m * FEATURES:(m + 1) * FEATURES] = out[r * BLOCK:(r + 1) * BLOCK]


def body(query_matrix, key_matrix, value_matrix, block_lists):
    pair = (2, GROUPS, PER_GROUP * BLOCK)
    return pl.pallas_call(
        kernel,
        out_shape=pltpu.VMEM((ROWS, HEADS * FEATURES), jnp.float32),
        in_specs=[pl.BlockSpec(memory_space=pl.ANY)] * 3 + [pl.BlockSpec(memory_space=pltpu.SMEM)],
        out_specs=pl.BlockSpec(memory_space=pltpu.VMEM),
        scratch_shapes=[
            pltpu.VMEM((BUFFERS, ROWS, COLS), jnp.float32),
            pltpu.VMEM((ROWS, HEADS * FEATURES), jnp.float32),
            pltpu.VMEM(pair + (256,), jnp.bfloat16),
            pltpu.VMEM(pair + (FEATURES,), jnp.float32),
            pltpu.VMEM(pair + (128,), jnp.float32),
            pltpu.VMEM(pair + (128,), jnp.float32),
            pltpu.SemaphoreType.DMA((len(RULES), CHUNKS)),
            pltpu.SemaphoreType.DMA((BUFFERS, CHUNKS)),
            pltpu.SemaphoreType.DMA((3,)),
        ],
        compiler_params=pltpu.CompilerParams(collective_id=0, has_side_effects=True, vmem_limit_bytes=56 << 20),
    )(query_matrix, key_matrix, value_matrix, block_lists)


def solution(mesh):
    spec = P(("ctxhi", "ctxlo"), None)
    return jax.shard_map(body, mesh=mesh, in_specs=(spec,) * 4, out_specs=spec, check_vma=False)
```

```python
import jax
import jax.numpy as jnp
from jax import lax
from jax.experimental import pallas as pl
from jax.experimental.pallas import tpu as pltpu
from jax.sharding import PartitionSpec as P

HEADS, GROUPS, FEATURES, BLOCK = 12, 2, 128, 128
PER_GROUP = HEADS // GROUPS
SLOTS = 15
ROWS, COLS = 256, 512
OFFSETS = (1, 2, 4, 8, 16, 32, 64, 128, 256)
OWN = 0
SLOT = {o: i + 1 for i, o in enumerate(OFFSETS)}
RELAY_Z, RELAY_Y = 10, 11
BUFFERS = 12
RULES = ("1", "2", "2b", "4", "4f", "4a", "8", "16", "32", "64", "128", "256", "256a")
CHUNKS = 8
CHUNK = ROWS // CHUNKS
Z_BACK = (4, 6, 2, 8, 8, 8, 2, 6)
Y_BACK = 5
STAGES = (("8", 1), ("64", 1), ("1", 1), ("own 32", 2), ("32", 9), ("y", 9), ("128", 9), ("z", 9), ("2", 9))
TURNS = 21
WORK = {0: 0, 4: 1, 6: 2, 8: 3, 10: 4, 12: 5, 14: 6, **{t: t - 9 for t in range(16, TURNS)}}
NEG = -1e30
MESH = pl.DeviceIdType.MESH

STEPS = (
    (1, (0, 0), (0, 1)), (0, (0, 0), (8, 0)), (0, (1, 0), (64, 0)), (1, (1, 0), (1, 1)), (1, (8, 1), (64, 1)), (0, (1, 1), (128, 0)),
    (0, (2, 0), (32, 0)), (1, (2, 1), (128, 1)), (0, (2, 1), (16, 0)), (1, (32, 1), (16, 1)), (0, (4, 0), (256, 0)), (1, (4, 1), (256, 1)),
)


def pick(index, values):
    out = jnp.int32(values[0])
    for i, v in enumerate(values[1:], 1):
        if v != values[i - 1]:
            out = jnp.where(index >= i, jnp.int32(v), out)
    return out


def split(a):
    hi = a.astype(jnp.bfloat16)
    return hi, (a - hi.astype(jnp.float32)).astype(jnp.bfloat16)


def kernel(q_ref, k_ref, v_ref, lists_ref, out_ref, buf, q_vmem, q_cat, acc, top, total, ssem, rsem, lsem):
    lo, hi = lax.axis_index("ctxlo"), lax.axis_index("ctxhi")
    h, z = lo // 8, lo % 8
    y, g, c = hi // 4, (hi // 2) % 2, hi % 2
    x = h * 2 + g
    shard = hi * 16 + lo

    def dev(dy, dx, dz, core):
        xx = (x + dx + 4) % 4
        return {"ctxlo": (xx // 2) * 8 + (z + dz + 8) % 8, "ctxhi": ((y + dy + 8) % 8) * 4 + (xx % 2) * 2 + core}

    k_copy = pltpu.make_async_copy(k_ref, buf.at[OWN, :, pl.ds(0, 256)], lsem.at[0])
    v_copy = pltpu.make_async_copy(v_ref, buf.at[OWN, :, pl.ds(256, 256)], lsem.at[1])
    q_copy = pltpu.make_async_copy(q_ref, q_vmem, lsem.at[2])
    k_copy.start()
    v_copy.start()
    q_copy.start()
    barrier = pltpu.get_barrier_semaphore()
    f = 1 - c
    peers = [dev(0, 0, 1, c), dev(0, 0, -1, c), dev(0, 0, 2, c), dev(0, 0, -2, c), dev(1, 0, 0, c), dev(-1, 0, 0, c),
             dev(2, 0, 0, c), dev(-2, 0, 0, c), dev(0, 1, 0, c), dev(0, -1, 0, c), dev(0, 1, 0, f), dev(0, -1, 0, f),
             dev(0, 2, 0, c), dev(0, 2, 0, f), dev(0, 0, 0, f)]
    for peer in peers:
        pl.semaphore_signal(barrier, 1, device_id=peer, device_id_type=MESH)
    k_copy.wait()
    v_copy.wait()
    pl.semaphore_wait(barrier, len(peers))

    def rows(k):
        return pl.ds(pl.multiple_of(k * CHUNK, CHUNK), CHUNK)

    def send(rule, src, dst, k, target):
        return pltpu.make_async_remote_copy(
            src_ref=buf.at[src, rows(k)], dst_ref=buf.at[dst, rows(k)],
            send_sem=ssem.at[RULES.index(rule), k], recv_sem=rsem.at[dst, k],
            device_id=target, device_id_type=MESH)

    def arrive(dst, k):
        send("1", dst, dst, k, peers[0]).wait_recv()

    t1, tz2, tzm2 = peers[0], peers[2], peers[3]

    def z_back(away):
        return pick(z, [Z_BACK[(i + away) % 8] for i in range(8)])

    back_own, back_relay, back_plus = z_back(0), z_back(2), z_back(-2)
    y1, y2, ym2 = peers[4], peers[6], peers[7]
    side = jnp.where(g == 0, 1, -1)
    t32 = dev(0, side, 0, c)
    t16 = dev(0, 0, 0, f)
    top_x = h == 1
    carry = top_x & (c == 1)
    t8 = dev(0, jnp.where(carry, -side, 2), 0, jnp.where(top_x, f, c))
    g1 = g == 1
    y8 = g1 & carry
    z_high = z >= 4
    no = jnp.logical_not

    def when(condition, action):
        pl.when(condition)(action)

    def own(rule, dst, target, condition=None):
        def go(k):
            if condition is None:
                send(rule, OWN, dst, k, target).start()
            else:
                when(condition(k), lambda: send(rule, OWN, dst, k, target).start())
        return go

    own_32 = own("32", SLOT[32], t32, lambda k: no(g1))
    for go in (own("1", SLOT[1], t1, lambda k: z < 7), own("4a", RELAY_Z, tzm2, lambda k: (k < back_own) & no(z_high)),
               own("8", SLOT[8], t8, lambda k: no(y8)), own("64", SLOT[64], y1),
               own("16", SLOT[16], t16, lambda k: c == 0), own("256a", RELAY_Y, ym2, lambda k: k < Y_BACK)):
        def first(k, _, go=go):
            go(k)
            return 0
        lax.fori_loop(0, CHUNKS, first, 0)

    def s64(k):
        arrive(SLOT[64], k)
        send("128", SLOT[64], SLOT[128], k, y1).start()
        when(y8, lambda: send("8", SLOT[64], SLOT[8], k, t8).start())
        when(g1, lambda: send("32", SLOT[64], SLOT[32], k, t32).start())

    def s32(k):
        arrive(SLOT[32], k)
        when(c == 1, lambda: send("16", SLOT[32], SLOT[16], k, t16).start())

    def s8(k):
        arrive(SLOT[8], k)
        when(z == 6, lambda: send("2b", SLOT[8], SLOT[2], k, tz2).start())
        when(z == 7, lambda: send("1", SLOT[8], SLOT[1], k, t1).start())
        when((k < back_own) & z_high, lambda: send("4a", SLOT[8], RELAY_Z, k, tzm2).start())

    def s1(k):
        arrive(SLOT[1], k)
        when(z < 7, lambda: send("2", SLOT[1], SLOT[2], k, t1).start())

    def s2(k):
        arrive(SLOT[2], k)
        when(k >= back_plus, lambda: send("4", SLOT[2], SLOT[4], k, tz2).start())

    def sz(k):
        @pl.when(k < back_relay)
        def _():
            arrive(RELAY_Z, k)
            send("4f", RELAY_Z, SLOT[4], k, tzm2).start()

    def s128(k):
        arrive(SLOT[128], k)
        when(k >= Y_BACK, lambda: send("256", SLOT[128], SLOT[256], k, y2).start())

    def sy(k):
        @pl.when(k < Y_BACK)
        def _():
            arrive(RELAY_Y, k)
            send("256", RELAY_Y, SLOT[256], k, ym2).start()

    stage = {"64": s64, "8": s8, "1": s1, "2": s2, "z": sz, "128": s128, "y": sy, "32": s32, "own 32": own_32}

    q_copy.wait()
    scale = jnp.float32(FEATURES ** -0.5 * 1.4426950408889634)
    for b in range(2):
        for n in range(HEADS):
            part = q_vmem[b * BLOCK:(b + 1) * BLOCK, n * FEATURES:(n + 1) * FEATURES] * scale
            high, low = split(part)
            at = pl.ds((n % PER_GROUP) * BLOCK, BLOCK)
            q_cat[b, n // PER_GROUP, at, 0:FEATURES] = high
            q_cat[b, n // PER_GROUP, at, FEATURES:] = low
    acc[...] = jnp.zeros_like(acc)
    total[...] = jnp.zeros_like(total)
    top[...] = jnp.full_like(top, NEG)

    col = lax.broadcasted_iota(jnp.int32, (BLOCK, 256), 1)
    row = lax.broadcasted_iota(jnp.int32, (BLOCK, 256), 0)

    def wait_all(offsets, start=0, stop=CHUNKS):
        def body(k, _):
            for o in offsets:
                arrive(SLOT[o], k)
            return 0
        lax.fori_loop(start, stop, body, 0)

    def step(i):
        b = pick(i, [s[0] for s in STEPS])
        where = []
        distance = []
        for p in (1, 2):
            o = pick(i, [s[p][0] for s in STEPS])
            slot = pick(i, [SLOT.get(s[p][0], OWN) for s in STEPS])
            kb = pick(i, [s[p][1] for s in STEPS])
            where.append((slot, pl.ds(pl.multiple_of(kb * BLOCK, BLOCK), BLOCK)))
            distance.append(2 * o + b - kb)
        away = jnp.where(col < BLOCK, distance[0], distance[1])
        target = shard * 2 + b - away
        hit = target[0:8] == lists_ref[b, 0]
        for m in range(1, SLOTS):
            hit = hit | (target[0:8] == lists_ref[b, m])
        bias8 = jnp.where(hit & (target[0:8] >= 0), jnp.float32(0), jnp.float32(NEG))
        bias = jnp.where((away > 0) | (col % BLOCK <= row), jnp.broadcast_to(bias8[0:1], (BLOCK, 256)), jnp.float32(NEG))

        ahead = []
        for n in range(GROUPS):
            def lanes(start, n=n):
                return pl.ds(start + n * FEATURES, FEATURES)

            keys = jnp.concatenate([buf[s, r, lanes(0)] for s, r in where], axis=0)
            values = jnp.concatenate([buf[s, r, lanes(256)] for s, r in where], axis=0)
            k_high, k_low = split(keys)
            v_high, v_low = split(values)
            k_cat = jnp.concatenate([k_high, k_high, k_low, k_low], axis=1)
            v_both = jnp.concatenate([v_high, v_low], axis=1)
            v_cat = jnp.concatenate([v_both, v_both], axis=0)
            dims = (((1,), (1,)), ((), ()))
            q = q_cat[b, n]
            scores = lax.dot_general(jnp.concatenate([q, q], axis=1), k_cat, dims, preferred_element_type=jnp.float32)
            scores = (scores.reshape(PER_GROUP, BLOCK, 256) + bias[None]).reshape(PER_GROUP * BLOCK, 256)
            ahead.append((scores, v_cat))
        for n, (scores, v_cat) in enumerate(ahead):
            old = top[b, n]
            new = jnp.maximum(old, jnp.max(scores, axis=1, keepdims=True))
            weights = jnp.exp2(scores - jnp.concatenate([new, new], axis=1))
            alpha = jnp.exp2(old - new)
            top[b, n] = new
            total[b, n] = total[b, n] * alpha + weights[:, :128] + weights[:, 128:]
            w_high, w_low = split(weights)
            o = jnp.dot(jnp.concatenate([w_high, w_low], axis=1), v_cat, preferred_element_type=jnp.float32)
            acc[b, n] = acc[b, n] * alpha + o[:, :128] + o[:, 128:]

    def finish(k, _):
        def sent(rule):
            send(rule, OWN, SLOT[64], k, t1).wait_send()
        for rule in ("64", "8", "1", "32", "16", "128", "256"):
            sent(rule)
        when(z < 7, lambda: sent("2"))
        when(z == 6, lambda: sent("2b"))
        when(k >= back_plus, lambda: sent("4"))
        when(k < back_relay, lambda: sent("4f"))
        when(k < back_own, lambda: sent("4a"))
        when(k < Y_BACK, lambda: sent("256a"))
        return 0

    def settle(b):
        for n in range(GROUPS):
            out = acc[b, n] * (1 / jnp.sum(total[b, n], axis=1, keepdims=True))
            for r in range(PER_GROUP):
                m = n * PER_GROUP + r
                out_ref[b * BLOCK:(b + 1) * BLOCK, m * FEATURES:(m + 1) * FEATURES] = out[r * BLOCK:(r + 1) * BLOCK]

    def turn(t, _):
        for name, start in STAGES:
            when((t >= start) & (t < start + CHUNKS), lambda name=name, start=start: stage[name](t - start))
        when(t == 17, lambda: wait_all((16,)))
        when(t == 19, lambda: wait_all((4, 256), 0, CHUNKS // 2))

        @pl.when(t == 20)
        def _():
            settle(0)
            lax.fori_loop(0, CHUNKS, finish, 0)
            wait_all((4, 256), CHUNKS // 2)

        half = pick(t, [WORK.get(i, -1) for i in range(TURNS)])

        @pl.when(half >= 0)
        def _():
            step(half)
        return 0

    lax.fori_loop(0, TURNS, turn, 0)

    settle(1)


def body(query_matrix, key_matrix, value_matrix, block_lists):
    pair = (2, GROUPS, PER_GROUP * BLOCK)
    return pl.pallas_call(
        kernel,
        out_shape=pltpu.VMEM((ROWS, HEADS * FEATURES), jnp.float32),
        in_specs=[pl.BlockSpec(memory_space=pl.ANY)] * 3 + [pl.BlockSpec(memory_space=pltpu.SMEM)],
        out_specs=pl.BlockSpec(memory_space=pltpu.VMEM),
        scratch_shapes=[
            pltpu.VMEM((BUFFERS, ROWS, COLS), jnp.float32),
            pltpu.VMEM((ROWS, HEADS * FEATURES), jnp.float32),
            pltpu.VMEM(pair + (256,), jnp.bfloat16),
            pltpu.VMEM(pair + (FEATURES,), jnp.float32),
            pltpu.VMEM(pair + (128,), jnp.float32),
            pltpu.VMEM(pair + (128,), jnp.float32),
            pltpu.SemaphoreType.DMA((len(RULES), CHUNKS)),
            pltpu.SemaphoreType.DMA((BUFFERS, CHUNKS)),
            pltpu.SemaphoreType.DMA((3,)),
        ],
        compiler_params=pltpu.CompilerParams(collective_id=0, has_side_effects=True, vmem_limit_bytes=56 << 20),
    )(query_matrix, key_matrix, value_matrix, block_lists)


def solution(mesh):
    spec = P(("ctxhi", "ctxlo"), None)
    return jax.shard_map(body, mesh=mesh, in_specs=(spec,) * 4, out_specs=spec, check_vma=False)
```

```python
import jax
import jax.numpy as jnp
from jax import lax
from jax.experimental import pallas as pl
from jax.experimental.pallas import tpu as pltpu
from jax.sharding import PartitionSpec as P

HEADS, GROUPS, FEATURES, BLOCK = 12, 2, 128, 128
PER_GROUP = HEADS // GROUPS
SLOTS = 15
ROWS, COLS = 256, 512
OFFSETS = (1, 2, 4, 8, 16, 32, 64, 128, 256)
OWN = 0
SLOT = {o: i + 1 for i, o in enumerate(OFFSETS)}
RELAY_Z, RELAY_Y = 10, 11
BUFFERS = 12
RULES = ("1", "2", "2b", "4", "4f", "4a", "8", "16", "32", "64", "128", "256", "256a")
CHUNKS = 8
CHUNK = ROWS // CHUNKS
Z_BACK = (4, 6, 2, 8, 8, 8, 2, 6)
Y_BACK = 5
STAGES = (("64", 1), ("8", 1), ("1", 1), ("own 32", 2), ("32", 9), ("y", 9), ("128", 9), ("z", 9), ("2", 9))
TURNS = 21
WORK = {0: 0, 4: 1, 6: 2, 8: 3, 10: 4, 12: 5, 14: 6, **{t: t - 9 for t in range(16, TURNS)}}
NEG = -1e30
MESH = pl.DeviceIdType.MESH

STEPS = (
    (1, (0, 0), (0, 1)), (0, (0, 0), (8, 0)), (0, (1, 0), (64, 0)), (1, (1, 0), (1, 1)), (1, (8, 1), (64, 1)), (0, (1, 1), (128, 0)),
    (0, (2, 0), (32, 0)), (1, (2, 1), (128, 1)), (0, (2, 1), (16, 0)), (1, (32, 1), (16, 1)), (0, (4, 0), (256, 0)), (1, (4, 1), (256, 1)),
)


def pick(index, values):
    out = jnp.int32(values[0])
    for i, v in enumerate(values[1:], 1):
        if v != values[i - 1]:
            out = jnp.where(index >= i, jnp.int32(v), out)
    return out


def split(a):
    hi = a.astype(jnp.bfloat16)
    return hi, (a - hi.astype(jnp.float32)).astype(jnp.bfloat16)


def kernel(q_ref, k_ref, v_ref, lists_ref, out_ref, buf, q_vmem, q_cat, acc, top, total, ssem, rsem, lsem):
    lo, hi = lax.axis_index("ctxlo"), lax.axis_index("ctxhi")
    h, z = lo // 8, lo % 8
    y, g, c = hi // 4, (hi // 2) % 2, hi % 2
    x = h * 2 + g
    shard = hi * 16 + lo

    def dev(dy, dx, dz, core):
        xx = (x + dx + 4) % 4
        return {"ctxlo": (xx // 2) * 8 + (z + dz + 8) % 8, "ctxhi": ((y + dy + 8) % 8) * 4 + (xx % 2) * 2 + core}

    k_copy = pltpu.make_async_copy(k_ref, buf.at[OWN, :, pl.ds(0, 256)], lsem.at[0])
    v_copy = pltpu.make_async_copy(v_ref, buf.at[OWN, :, pl.ds(256, 256)], lsem.at[1])
    q_copy = pltpu.make_async_copy(q_ref, q_vmem, lsem.at[2])
    k_copy.start()
    v_copy.start()
    q_copy.start()
    barrier = pltpu.get_barrier_semaphore()
    f = 1 - c
    peers = [dev(0, 0, 1, c), dev(0, 0, -1, c), dev(0, 0, 2, c), dev(0, 0, -2, c), dev(1, 0, 0, c), dev(-1, 0, 0, c),
             dev(2, 0, 0, c), dev(-2, 0, 0, c), dev(0, 1, 0, c), dev(0, -1, 0, c), dev(0, 1, 0, f), dev(0, -1, 0, f),
             dev(0, 2, 0, c), dev(0, 2, 0, f), dev(0, 0, 0, f)]
    for peer in peers:
        pl.semaphore_signal(barrier, 1, device_id=peer, device_id_type=MESH)
    k_copy.wait()
    v_copy.wait()
    pl.semaphore_wait(barrier, len(peers))

    def rows(k):
        return pl.ds(pl.multiple_of(k * CHUNK, CHUNK), CHUNK)

    def send(rule, src, dst, k, target):
        return pltpu.make_async_remote_copy(
            src_ref=buf.at[src, rows(k)], dst_ref=buf.at[dst, rows(k)],
            send_sem=ssem.at[RULES.index(rule), k], recv_sem=rsem.at[dst, k],
            device_id=target, device_id_type=MESH)

    def arrive(dst, k):
        send("1", dst, dst, k, peers[0]).wait_recv()

    t1, tz2, tzm2 = peers[0], peers[2], peers[3]

    def z_back(away):
        return pick(z, [Z_BACK[(i + away) % 8] for i in range(8)])

    back_own, back_relay, back_plus = z_back(0), z_back(2), z_back(-2)
    y1, y2, ym2 = peers[4], peers[6], peers[7]
    side = jnp.where(g == 0, 1, -1)
    t32 = dev(0, side, 0, c)
    t16 = dev(0, 0, 0, f)
    top_x = h == 1
    carry = top_x & (c == 1)
    t8 = dev(0, jnp.where(carry, -side, 2), 0, jnp.where(top_x, f, c))
    g1 = g == 1
    y8 = g1 & carry
    z_high = z >= 4
    no = jnp.logical_not

    def when(condition, action):
        pl.when(condition)(action)

    def own(rule, dst, target, condition=None):
        def go(k):
            if condition is None:
                send(rule, OWN, dst, k, target).start()
            else:
                when(condition(k), lambda: send(rule, OWN, dst, k, target).start())
        return go

    own_32 = own("32", SLOT[32], t32, lambda k: no(g1))
    for go in (own("1", SLOT[1], t1, lambda k: z < 7), own("4a", RELAY_Z, tzm2, lambda k: (k < back_own) & no(z_high)),
               own("8", SLOT[8], t8, lambda k: no(y8)), own("64", SLOT[64], y1),
               own("16", SLOT[16], t16, lambda k: c == 0), own("256a", RELAY_Y, ym2, lambda k: k < Y_BACK)):
        def first(k, _, go=go):
            go(k)
            return 0
        lax.fori_loop(0, CHUNKS, first, 0)

    def s64(k):
        arrive(SLOT[64], k)
        send("128", SLOT[64], SLOT[128], k, y1).start()
        when(y8, lambda: send("8", SLOT[64], SLOT[8], k, t8).start())
        when(g1, lambda: send("32", SLOT[64], SLOT[32], k, t32).start())

    def s32(k):
        arrive(SLOT[32], k)
        when(c == 1, lambda: send("16", SLOT[32], SLOT[16], k, t16).start())

    def s8(k):
        arrive(SLOT[8], k)
        when(z == 6, lambda: send("2b", SLOT[8], SLOT[2], k, tz2).start())
        when(z == 7, lambda: send("1", SLOT[8], SLOT[1], k, t1).start())
        when((k < back_own) & z_high, lambda: send("4a", SLOT[8], RELAY_Z, k, tzm2).start())

    def s1(k):
        arrive(SLOT[1], k)
        when(z < 7, lambda: send("2", SLOT[1], SLOT[2], k, t1).start())

    def s2(k):
        arrive(SLOT[2], k)
        when(k >= back_plus, lambda: send("4", SLOT[2], SLOT[4], k, tz2).start())

    def sz(k):
        @pl.when(k < back_relay)
        def _():
            arrive(RELAY_Z, k)
            send("4f", RELAY_Z, SLOT[4], k, tzm2).start()

    def s128(k):
        arrive(SLOT[128], k)
        when(k >= Y_BACK, lambda: send("256", SLOT[128], SLOT[256], k, y2).start())

    def sy(k):
        @pl.when(k < Y_BACK)
        def _():
            arrive(RELAY_Y, k)
            send("256", RELAY_Y, SLOT[256], k, ym2).start()

    stage = {"64": s64, "8": s8, "1": s1, "2": s2, "z": sz, "128": s128, "y": sy, "32": s32, "own 32": own_32}

    q_copy.wait()
    scale = jnp.float32(FEATURES ** -0.5 * 1.4426950408889634)
    for b in range(2):
        for n in range(HEADS):
            part = q_vmem[b * BLOCK:(b + 1) * BLOCK, n * FEATURES:(n + 1) * FEATURES] * scale
            high, low = split(part)
            at = pl.ds((n % PER_GROUP) * BLOCK, BLOCK)
            q_cat[b, n // PER_GROUP, at, 0:FEATURES] = high
            q_cat[b, n // PER_GROUP, at, FEATURES:] = low
    acc[...] = jnp.zeros_like(acc)
    total[...] = jnp.zeros_like(total)
    top[...] = jnp.full_like(top, NEG)

    col = lax.broadcasted_iota(jnp.int32, (BLOCK, 256), 1)
    row = lax.broadcasted_iota(jnp.int32, (BLOCK, 256), 0)

    def wait_all(offsets, start=0, stop=CHUNKS):
        def body(k, _):
            for o in offsets:
                arrive(SLOT[o], k)
            return 0
        lax.fori_loop(start, stop, body, 0)

    def step(i):
        b = pick(i, [s[0] for s in STEPS])
        where = []
        distance = []
        for p in (1, 2):
            o = pick(i, [s[p][0] for s in STEPS])
            slot = pick(i, [SLOT.get(s[p][0], OWN) for s in STEPS])
            kb = pick(i, [s[p][1] for s in STEPS])
            where.append((slot, pl.ds(pl.multiple_of(kb * BLOCK, BLOCK), BLOCK)))
            distance.append(2 * o + b - kb)
        away = jnp.where(col < BLOCK, distance[0], distance[1])
        target = shard * 2 + b - away
        hit = target[0:8] == lists_ref[b, 0]
        for m in range(1, SLOTS):
            hit = hit | (target[0:8] == lists_ref[b, m])
        bias8 = jnp.where(hit & (target[0:8] >= 0), jnp.float32(0), jnp.float32(NEG))
        bias = jnp.where((away > 0) | (col % BLOCK <= row), jnp.broadcast_to(bias8[0:1], (BLOCK, 256)), jnp.float32(NEG))

        ahead = []
        for n in range(GROUPS):
            def lanes(start, n=n):
                return pl.ds(start + n * FEATURES, FEATURES)

            keys = jnp.concatenate([buf[s, r, lanes(0)] for s, r in where], axis=0)
            values = jnp.concatenate([buf[s, r, lanes(256)] for s, r in where], axis=0)
            k_high, k_low = split(keys)
            v_high, v_low = split(values)
            k_cat = jnp.concatenate([k_high, k_high, k_low, k_low], axis=1)
            v_both = jnp.concatenate([v_high, v_low], axis=1)
            v_cat = jnp.concatenate([v_both, v_both], axis=0)
            dims = (((1,), (1,)), ((), ()))
            q = q_cat[b, n]
            scores = lax.dot_general(jnp.concatenate([q, q], axis=1), k_cat, dims, preferred_element_type=jnp.float32)
            scores = (scores.reshape(PER_GROUP, BLOCK, 256) + bias[None]).reshape(PER_GROUP * BLOCK, 256)
            ahead.append((scores, v_cat))
        for n, (scores, v_cat) in enumerate(ahead):
            old = top[b, n]
            new = jnp.maximum(old, jnp.max(scores, axis=1, keepdims=True))
            weights = jnp.exp2(scores - jnp.concatenate([new, new], axis=1))
            alpha = jnp.exp2(old - new)
            top[b, n] = new
            total[b, n] = total[b, n] * alpha + weights[:, :128] + weights[:, 128:]
            w_high, w_low = split(weights)
            o = jnp.dot(jnp.concatenate([w_high, w_low], axis=1), v_cat, preferred_element_type=jnp.float32)
            acc[b, n] = acc[b, n] * alpha + o[:, :128] + o[:, 128:]

    def finish(k, _):
        def sent(rule):
            send(rule, OWN, SLOT[64], k, t1).wait_send()
        for rule in ("64", "8", "1", "32", "16", "128", "256"):
            sent(rule)
        when(z < 7, lambda: sent("2"))
        when(z == 6, lambda: sent("2b"))
        when(k >= back_plus, lambda: sent("4"))
        when(k < back_relay, lambda: sent("4f"))
        when(k < back_own, lambda: sent("4a"))
        when(k < Y_BACK, lambda: sent("256a"))
        return 0

    def settle(b):
        for n in range(GROUPS):
            out = acc[b, n] * (1 / jnp.sum(total[b, n], axis=1, keepdims=True))
            for r in range(PER_GROUP):
                m = n * PER_GROUP + r
                out_ref[b * BLOCK:(b + 1) * BLOCK, m * FEATURES:(m + 1) * FEATURES] = out[r * BLOCK:(r + 1) * BLOCK]

    def turn(t, _):
        for name, start in STAGES:
            when((t >= start) & (t < start + CHUNKS), lambda name=name, start=start: stage[name](t - start))
        when(t == 17, lambda: wait_all((16,)))
        when(t == 19, lambda: wait_all((4, 256), 0, CHUNKS // 2))

        @pl.when(t == 20)
        def _():
            settle(0)
            lax.fori_loop(0, CHUNKS, finish, 0)
            wait_all((4, 256), CHUNKS // 2)

        half = pick(t, [WORK.get(i, -1) for i in range(TURNS)])

        @pl.when(half >= 0)
        def _():
            step(half)
        return 0

    lax.fori_loop(0, TURNS, turn, 0)

    settle(1)


def body(query_matrix, key_matrix, value_matrix, block_lists):
    pair = (2, GROUPS, PER_GROUP * BLOCK)
    return pl.pallas_call(
        kernel,
        out_shape=pltpu.VMEM((ROWS, HEADS * FEATURES), jnp.float32),
        in_specs=[pl.BlockSpec(memory_space=pl.ANY)] * 3 + [pl.BlockSpec(memory_space=pltpu.SMEM)],
        out_specs=pl.BlockSpec(memory_space=pltpu.VMEM),
        scratch_shapes=[
            pltpu.VMEM((BUFFERS, ROWS, COLS), jnp.float32),
            pltpu.VMEM((ROWS, HEADS * FEATURES), jnp.float32),
            pltpu.VMEM(pair + (256,), jnp.bfloat16),
            pltpu.VMEM(pair + (FEATURES,), jnp.float32),
            pltpu.VMEM(pair + (128,), jnp.float32),
            pltpu.VMEM(pair + (128,), jnp.float32),
            pltpu.SemaphoreType.DMA((len(RULES), CHUNKS)),
            pltpu.SemaphoreType.DMA((BUFFERS, CHUNKS)),
            pltpu.SemaphoreType.DMA((3,)),
        ],
        compiler_params=pltpu.CompilerParams(collective_id=0, has_side_effects=True, vmem_limit_bytes=56 << 20),
    )(query_matrix, key_matrix, value_matrix, block_lists)


def solution(mesh):
    spec = P(("ctxhi", "ctxlo"), None)
    return jax.shard_map(body, mesh=mesh, in_specs=(spec,) * 4, out_specs=spec, check_vma=False)
```
